256 devices in a mesh: tp: 8 (over y_lo, x), ep: 32 (over y_hi, z, core).
Axes of the slice: x: 4, y: 4 (y_hi: 2, y_lo: 2; y = y_hi * 2 + y_lo), z: 8, core: 2. Of those that a mesh axis runs over, the one named last changes fastest.
Arguments:
- tokens: bfloat16 [4096, 3584], P(('ep', 'tp')), may hold values from -6 to 6
- norm_gain: float32 [3584], replicated, may hold values from 0.1 to 1.9
- dense_gate: bfloat16 [3584, 2432], P('ep', 'tp'), may hold values from -0.09375 to 0.09375
- dense_up: bfloat16 [3584, 2432], P('ep', 'tp'), may hold values from -0.09375 to 0.09375
- dense_down: bfloat16 [2432, 3584], P('tp', 'ep'), may hold values from -0.125 to 0.125
- expert_gate: bfloat16 [32, 3584, 2432], P('ep', None, 'tp'), may hold values from -0.09375 to 0.09375
- expert_up: bfloat16 [32, 3584, 2432], P('ep', None, 'tp'), may hold values from -0.09375 to 0.09375
- expert_down: bfloat16 [32, 2432, 3584], P('ep', 'tp'), may hold values from -0.125 to 0.125
- expert_ids: int32 [4096, 2], P('ep'), may hold values from 0 to 31, all different within a row; in each aligned block of 128 rows (0 to 127, 128 to 255, ...) at most 16 rows name the same one
- gate_weights: float32 [4096, 2], P('ep'), may hold values from 0.1 to 1
- cotangent: bfloat16 [4096, 3584], P(('ep', 'tp')), may hold values from -6 to 6
Outputs:
- mixed: bfloat16 [4096, 3584], P(('ep', 'tp'))
- input_grad: bfloat16 [4096, 3584], P(('ep', 'tp'))
The draws below stay inside these ranges and needn't reach their ends.
Inputs may be any that keep to these rules, and one draw needn't show every extreme that they name: `expert_ids`: A token's two experts differ. In each block of 128 consecutive tokens no expert is named by more than 16 routes, a bound that some block reaches; every expert is named somewhere.
All inputs are finite; a program needn't handle non-finite values.
Results may differ from the reference program's by a relative error of at most 0.018.
Values may be sent and summed in bfloat16 or wider, within the bound.
No kernel may reach another device: no remote copies, remote signals or barrier semaphores. Data moves between devices by JAX's collectives and lax.ppermute only.
A program may use at most 128 MiB of HBM per device.

```python
import math
import jax
import jax.numpy as jnp
import numpy as np
from jax import lax

D = 3584
FFD = 2432
FE = 2432
TOK_EP = 128
EXPERTS = 32
CAP = 16
TOKENS = 4096
N_TP = 8


def steps_of(stream_key, extent, split, least, largest):
    loudness = 1.0
    for dim, blocks in split:
        heights = jax.random.uniform(jax.random.fold_in(jax.random.fold_in(stream_key, 6), dim), (blocks,), jnp.float32, least / len(split), largest / len(split))
        loudness = loudness * jnp.repeat(jnp.exp(heights), extent[dim] // blocks).reshape((-1,) + (1,) * (len(extent) - 1 - dim))
    return loudness


def shared_out(rng, own, number, rows, count, top, bound, lean):
    sequence = jax.random.permutation(rng, count)
    heavy_load, common = shares(count, rows * top, bound, lean, True), shares(count, rows * top, bound, lean, False)
    places = jnp.arange(count)

    def named(tallies, turn):
        used = int((tallies > 0).sum())
        fixed = max(1, used // 4)
        passed = fixed + (places - fixed + turn * (used - fixed)) % max(1, count - fixed)
        return jnp.zeros((count,), jnp.int32).at[sequence[jnp.where(places < fixed, places, passed)]].set(jnp.asarray(tallies, jnp.int32))

    tallies = jnp.where(number % 4 == 0, named(heavy_load, number // 4), named(common, number - number // 4 - 1))
    mixed = jax.random.permutation(jax.random.fold_in(own, 3), count)
    giver, receiver = mixed[0:count // 2 * 2:2], mixed[1:count // 2 * 2:2]
    slack = jnp.minimum(tallies[giver] - 1, bound - tallies[receiver]) // 2
    slack = jnp.where((giver == sequence[0]) | (receiver == sequence[0]) | (tallies[receiver] == 0), 0, jnp.maximum(slack, 0))
    passed = jax.random.randint(jax.random.fold_in(own, 4), (count // 2,), 0, 1 << 20) % (slack + 1)
    tallies = tallies.at[giver].add(-passed).at[receiver].add(passed)
    labels = jnp.searchsorted(jnp.cumsum(tallies), jnp.arange(rows * top), side="right").astype(jnp.int32)
    grid = labels.reshape(top, rows).T
    grid = grid[jax.random.permutation(jax.random.fold_in(own, 1), rows)]
    turn = jax.random.randint(jax.random.fold_in(own, 2), (rows, 1), 0, top)
    return jnp.take_along_axis(grid, (jnp.arange(top)[None, :] + turn) % top, axis=1)


def shares(number_of, total, bound, skew, full):
    portions = [(1 << 20) // math.isqrt(rank ** skew) + 1 for rank in range(1, number_of + 1)]
    largest = bound if full else min(bound, max(-(-total // number_of), total * portions[0] // sum(portions)))
    least = 1 if total - largest >= number_of - 1 else 0
    holding, surplus = [largest] + [least] * (number_of - 1), total - largest - least * (number_of - 1)
    while surplus > 0:
        movable = [i for i in range(1, number_of) if holding[i] < largest] or [i for i in range(1, number_of) if holding[i] < bound]
        mass, remaining = sum([portions[i] for i in movable]), surplus
        for i in movable:
            extra = min(bound - holding[i], max(1, remaining * portions[i] // mass), surplus)
            holding[i] = holding[i] + extra
            surplus = surplus - extra
    return np.array(holding)


def scatter_about(stream_key, dims, spread, limit, split=(), held_as=jnp.bfloat16):
    result = jax.random.normal(stream_key, dims, jnp.float32) * spread
    if len(split) > 0:
        result = steps_of(stream_key, dims, split, -0.22, 0.18) * result
    return jnp.clip(result, min=-limit, max=limit).astype(held_as)


def setup_inputs(seed: int = 0) -> dict:
    splits = jax.random.split(jax.random.key(seed), 12)
    tokens = scatter_about(splits[0], (TOKENS, D), 1.0, 6.0, ((0, 256),))
    norm_gain = jnp.clip(1.0 + 0.18 * jax.random.normal(splits[1], (D,), jnp.float32), 0.1, 1.9)
    dense_gate = scatter_about(splits[2], (D, FFD), D ** -0.5, 0.09375, ((0, 32), (1, 8)))
    dense_up = scatter_about(splits[3], (D, FFD), D ** -0.5, 0.09375, ((0, 32), (1, 8)))
    dense_down = scatter_about(splits[4], (FFD, D), FFD ** -0.5, 0.125, ((0, 8), (1, 32)))
    expert_gate = scatter_about(splits[5], (EXPERTS, D, FE), D ** -0.5, 0.09375, ((0, 32), (2, 8)))
    expert_up = scatter_about(splits[6], (EXPERTS, D, FE), D ** -0.5, 0.09375, ((0, 32), (2, 8)))
    expert_down = scatter_about(splits[7], (EXPERTS, FE, D), FE ** -0.5, 0.125, ((0, 32), (1, 8)))
    expert_ids_keys = jax.random.split(jax.random.fold_in(splits[8], 1), TOKENS // TOK_EP)
    expert_ids_turns = jax.random.permutation(jax.random.fold_in(splits[8], 3), TOKENS // TOK_EP)
    expert_ids = jax.vmap(lambda own, number: shared_out(jax.random.fold_in(splits[8], 2), own, number, TOK_EP, EXPERTS, 2, CAP, 2))(expert_ids_keys, expert_ids_turns).reshape((TOKENS, 2))
    gate_weights = jnp.clip(0.1 + 0.9 * jax.random.uniform(splits[9], (TOKENS, 2), jnp.float32) ** steps_of(splits[9], (TOKENS, 2), ((0, 32),), -0.2, 0.2), 0.1, 1.0)
    cotangent = scatter_about(splits[10], (TOKENS, D), 1.0, 6.0, ((0, 256),))
    return {"tokens": tokens, "norm_gain": norm_gain, "dense_gate": dense_gate, "dense_up": dense_up, "dense_down": dense_down, "expert_gate": expert_gate, "expert_up": expert_up, "expert_down": expert_down, "expert_ids": expert_ids, "gate_weights": gate_weights, "cotangent": cotangent}


norm_eps = 1e-05

def silu_parts(pre):
    sigma = jax.nn.sigmoid(pre)
    return (pre * sigma, sigma * (1.0 + pre * (1.0 - sigma)))

def matmul(left, right):
    return jnp.dot(left, right, preferred_element_type=jnp.float32)

def matmul_transposed(left, right):
    return lax.dot_general(left, right, (((1,), (1,)), ((), ())), preferred_element_type=jnp.float32)

def route_positions(group_ids, experts, capacity):
    route_expert = group_ids.reshape(-1).astype(jnp.int32)
    onehot = (route_expert[:, None] == jnp.arange(experts, dtype=jnp.int32)[None, :]).astype(jnp.int32)
    earlier = jnp.cumsum(onehot, axis=0, dtype=jnp.int32) - onehot
    slot_pos = lax.optimization_barrier(jnp.sum(earlier * onehot, axis=1, dtype=jnp.int32)).astype(jnp.int32)
    position = (route_expert * capacity + slot_pos).astype(jnp.int32)
    routes = route_expert.shape[0]
    route_table = jnp.full((experts * capacity,), routes, jnp.int32).at[position].set(jnp.arange(routes, dtype=jnp.int32))
    return (route_expert, slot_pos, position, route_table)

def pick_rows(source, lookup):
    return jnp.take(source, lookup, axis=0, mode='fill', fill_value=0)

def reference(tokens, norm_gain, dense_gate, dense_up, dense_down, expert_gate, expert_up, expert_down, expert_ids, gate_weights, cotangent):
    inputs = tokens.astype(jnp.float32)
    inverse = lax.rsqrt(lax.optimization_barrier(jnp.mean(inputs * inputs, axis=1, keepdims=True)) + norm_eps)
    scaled = inputs * inverse
    normed = (scaled * norm_gain).astype(jnp.bfloat16)
    gate_pre = matmul(normed, dense_gate)
    up_pre = matmul(normed, dense_up)
    active, slope = silu_parts(gate_pre)
    hidden = (active * up_pre).astype(jnp.bfloat16)
    dense_out = matmul(hidden, dense_down)
    hidden_cot = matmul_transposed(cotangent, dense_down)
    gate_cot = (hidden_cot * up_pre * slope).astype(jnp.bfloat16)
    up_cot = (hidden_cot * active).astype(jnp.bfloat16)
    dense_back = matmul_transposed(gate_cot, dense_gate) + matmul_transposed(up_cot, dense_up)
    groups = TOKENS // TOK_EP
    piece = FE // N_TP

    def group_table(group_ids):
        return route_positions(group_ids, EXPERTS, CAP)[3]
    route_table = jax.vmap(group_table)(expert_ids.reshape(groups, TOK_EP, 2)).reshape(groups, EXPERTS, CAP)
    normed_groups = normed.reshape(groups, TOK_EP, D)
    route_cot = (cotangent.astype(jnp.float32).reshape(groups, TOK_EP, 1, D) * gate_weights.reshape(groups, TOK_EP, 2, 1)).astype(jnp.bfloat16).reshape(groups, 2 * TOK_EP, D)
    weight_groups = gate_weights.reshape(groups, 2 * TOK_EP)
    group_index = jnp.arange(groups, dtype=jnp.int32)[:, None]

    def per_expert(carry, expert):
        forward_sum, backward_sum = carry
        lookup = route_table[:, expert, :]
        token_lookup = (lookup // 2).astype(jnp.int32)
        rows_in = jax.vmap(pick_rows)(normed_groups, token_lookup).reshape(groups * CAP, D)
        rows_cot = jax.vmap(pick_rows)(route_cot, lookup).reshape(groups * CAP, D)
        weights = jax.vmap(pick_rows)(weight_groups, lookup).reshape(groups * CAP, 1)
        local_gate = expert_gate[expert]
        local_up = expert_up[expert]
        local_down = expert_down[expert]
        expert_gate_pre = matmul(rows_in, local_gate)
        expert_up_pre = matmul(rows_in, local_up)
        expert_active, expert_slope = silu_parts(expert_gate_pre)
        expert_hidden = (expert_active * expert_up_pre).astype(jnp.bfloat16)
        parts = jnp.einsum('rgf,gfd->rgd', expert_hidden.reshape(-1, N_TP, piece).astype(jnp.float32), local_down.reshape(N_TP, piece, D).astype(jnp.float32))
        expert_out = lax.optimization_barrier(parts.astype(jnp.bfloat16)).astype(jnp.float32).sum(axis=1)
        forward_terms = (weights * expert_out).reshape(groups, CAP, D)
        forward_sum = forward_sum.at[group_index, token_lookup].add(forward_terms, mode='drop')
        expert_hidden_cot = matmul_transposed(rows_cot, local_down)
        expert_gate_cot = (expert_hidden_cot * expert_up_pre * expert_slope).astype(jnp.bfloat16)
        expert_up_cot = (expert_hidden_cot * expert_active).astype(jnp.bfloat16)
        back_parts = jnp.einsum('rgf,dgf->rgd', expert_gate_cot.reshape(-1, N_TP, piece).astype(jnp.float32), local_gate.reshape(D, N_TP, piece).astype(jnp.float32))
        back_parts = back_parts + jnp.einsum('rgf,dgf->rgd', expert_up_cot.reshape(-1, N_TP, piece).astype(jnp.float32), local_up.reshape(D, N_TP, piece).astype(jnp.float32))
        expert_back = lax.optimization_barrier(back_parts.astype(jnp.bfloat16)).astype(jnp.float32).sum(axis=1)
        backward_sum = backward_sum.at[group_index, token_lookup].add(expert_back.reshape(groups, CAP, D), mode='drop')
        return ((forward_sum, backward_sum), None)
    start = (jnp.zeros((groups, TOK_EP, D), jnp.float32), jnp.zeros((groups, TOK_EP, D), jnp.float32))
    carried = lax.scan(per_expert, start, jnp.arange(EXPERTS, dtype=jnp.int32))[0]
    moe_out = carried[0].reshape(TOKENS, D)
    mixed = (inputs + dense_out + moe_out).astype(jnp.bfloat16)
    normed_cot = (dense_back + carried[1].reshape(TOKENS, D)) * norm_gain
    input_grad = (cotangent.astype(jnp.float32) + inverse * (normed_cot - scaled * lax.optimization_barrier(jnp.mean(normed_cot * scaled, axis=1, keepdims=True)))).astype(jnp.bfloat16)
    return (mixed, input_grad)
```

```python
import jax
import jax.numpy as jnp
from jax import lax
from jax.sharding import PartitionSpec as P

norm_eps = 1e-05
bf16 = jnp.bfloat16
f32 = jnp.float32


def silu_parts(pre):
    sigma = jax.nn.sigmoid(pre)
    return (pre * sigma, sigma * (1.0 + pre * (1.0 - sigma)))


def matmul(left, right):
    return jnp.dot(left, right, preferred_element_type=f32)


def matmul_transposed(left, right):
    return lax.dot_general(left, right, (((1,), (1,)), ((), ())), preferred_element_type=f32)


def shift_x(array, step):
    return lax.ppermute(
        array, "tp", [(y * 4 + x, y * 4 + (x + step) % 4) for y in range(2) for x in range(4)]
    )


offsets = (0, -1, 1, 2)


def line(x):
    return [lax.rem(x + 4 + step, 4) for step in offsets]


def gather_x(own):
    half = own.shape[0] // 2
    low = shift_x(own, 1)
    high = shift_x(own, -1)
    far_a = shift_x(low[:half], 1)
    far_b = shift_x(high[half:], -1)
    return [own, low, high, jnp.concatenate([far_a, far_b], axis=0)]


def scatter_x(parts):
    own, low, high, far = parts
    half = own.shape[0] // 2
    from_high = shift_x(far[:half].astype(bf16), -1)
    from_low = shift_x(far[half:].astype(bf16), 1)
    low = jnp.concatenate([low[:half] + from_high.astype(f32), low[half:]], axis=0)
    high = jnp.concatenate([high[:half], high[half:] + from_low.astype(f32)], axis=0)
    return (
        own
        + shift_x(low.astype(bf16), -1).astype(f32)
        + shift_x(high.astype(bf16), 1).astype(f32)
    )


def in_line_order(blocks, x):
    order = line(x)
    return [
        lax.select_n(order[k], *blocks) for k in range(4)
    ]


def in_line_order_inverse(blocks, x):
    own, low, high, far = blocks
    by_offset = [own, high, far, low]
    return [lax.select_n(lax.rem(k + 4 - x, 4), *by_offset) for k in range(4)]


def exchange_tp(blocks):
    return lax.all_to_all(blocks, "tp", split_axis=0, concat_axis=0, tiled=True)


def exchange(rows):
    experts = lax.axis_size("ep")
    return lax.all_to_all(
        rows.reshape(experts, -1, rows.shape[1]), "ep", split_axis=0, concat_axis=0, tiled=True
    ).reshape(rows.shape)


def slots(expert_ids, experts):
    route_expert = expert_ids.reshape(-1)
    onehot = (route_expert[:, None] == jnp.arange(experts, dtype=jnp.int32)[None, :]).astype(f32)
    routes = route_expert.shape[0]
    before = jnp.tril(jnp.ones((routes, routes), f32), -1)
    earlier = matmul(before.astype(bf16), onehot.astype(bf16))
    slot = jnp.sum(earlier * onehot, axis=1).astype(jnp.int32)
    return route_expert.reshape(-1, 2), slot.reshape(-1, 2)


def body(
    tokens,
    norm_gain,
    dense_gate,
    dense_up,
    dense_down,
    expert_gate,
    expert_up,
    expert_down,
    expert_ids,
    gate_weights,
    cotangent,
):
    experts = lax.axis_size("ep")
    group_rows = expert_ids.shape[0]
    capacity = 4 * group_rows // experts
    hidden_units = dense_gate.shape[1]
    inputs = tokens.astype(f32)
    inverse = lax.rsqrt(jnp.mean(inputs * inputs, axis=1, keepdims=True) + norm_eps)
    scaled = inputs * inverse
    normed = (scaled * norm_gain).astype(bf16)

    dense_own = jnp.concatenate([dense_gate, dense_up, dense_down.T], axis=1)
    dense_full = lax.all_gather(dense_own, "ep", axis=0, tiled=True)

    me = lax.axis_index("tp")
    x = lax.rem(me, 4)
    width = tokens.shape[1] // 4

    def columns(array, k):
        return array[:, k * width : (k + 1) * width]

    pieces = jnp.stack(
        [
            jnp.concatenate([columns(normed, k), columns(cotangent, k)], axis=1)
            for k in range(4)
        ]
    )
    group = exchange_tp(jnp.concatenate([pieces, pieces], axis=0)).reshape(group_rows, -1)

    route_expert, slot = slots(expert_ids, experts)
    place = jnp.arange(experts * capacity, dtype=jnp.int32)[:, None]
    position = route_expert * capacity + slot
    pick, weight = None, None
    for k in range(2):
        chosen = position[None, :, k] == place
        chosen_weight = jnp.where(chosen, gate_weights[None, :, k], 0.0)
        pick = chosen if pick is None else pick | chosen
        weight = chosen_weight if weight is None else weight + chosen_weight
    weight = jnp.sum(weight, axis=1, keepdims=True)
    pick_f32 = pick.astype(f32)
    pick_bf16 = pick.astype(bf16)

    dense_rows = gather_x(group)

    rows_in = exchange(matmul(pick_bf16, group[:, :width]).astype(bf16))
    rows_cot = exchange((matmul(pick_bf16, group[:, width:]) * weight).astype(bf16))
    rows_in, dense_rows = lax.optimization_barrier((rows_in, dense_rows))
    rows_in = gather_x(rows_in)
    rows_cot, rows_in = lax.optimization_barrier((rows_cot, rows_in))
    rows_cot = gather_x(rows_cot)

    def row_blocks(array):
        return in_line_order([array[k * width : (k + 1) * width] for k in range(4)], x)

    local_gate, local_up = row_blocks(expert_gate[0]), row_blocks(expert_up[0])
    local_down = in_line_order([columns(expert_down[0], k) for k in range(4)], x)
    local_gate, local_up, local_down = lax.optimization_barrier(
        (local_gate, local_up, local_down)
    )

    def back(blocks):
        return exchange(scatter_x(blocks).astype(bf16)).astype(f32)

    expert_gate_pre = sum(matmul(rows_in[k], local_gate[k]) for k in range(4))
    expert_up_pre = sum(matmul(rows_in[k], local_up[k]) for k in range(4))
    expert_active, expert_slope = silu_parts(expert_gate_pre)
    expert_hidden = (expert_active * expert_up_pre).astype(bf16)
    expert_out = back([matmul(expert_hidden, local_down[k]) for k in range(4)])
    expert_hidden_cot = sum(matmul_transposed(rows_cot[k], local_down[k]) for k in range(4))
    expert_gate_cot = (expert_hidden_cot * expert_up_pre * expert_slope).astype(bf16)
    expert_up_cot = (expert_hidden_cot * expert_active).astype(bf16)
    expert_back = back(
        [
            matmul_transposed(expert_gate_cot, local_gate[k])
            + matmul_transposed(expert_up_cot, local_up[k])
            for k in range(4)
        ]
    )

    def to_tokens(slot_rows):
        return lax.dot_general(
            pick_f32,
            slot_rows,
            (((0,), (0,)), ((), ())),
            precision=lax.Precision.HIGHEST,
            preferred_element_type=f32,
        )

    dense_rows = jnp.concatenate(
        [
            jnp.concatenate([rows[:, :width], rows[:, width:]], axis=0)
            for rows in in_line_order_inverse(dense_rows, x)
        ],
        axis=1,
    )
    pre = matmul(dense_rows, dense_full)
    gate_pre = pre[:group_rows, :hidden_units]
    up_pre = pre[:group_rows, hidden_units : 2 * hidden_units]
    hidden_cot = pre[group_rows:, 2 * hidden_units :]
    active, slope = silu_parts(gate_pre)
    hidden = (active * up_pre).astype(bf16)
    gate_cot = (hidden_cot * up_pre * slope).astype(bf16)
    up_cot = (hidden_cot * active).astype(bf16)
    zeros = jnp.zeros_like(hidden)
    both = jnp.concatenate(
        [
            jnp.concatenate([zeros, zeros, hidden], axis=1),
            jnp.concatenate([gate_cot, up_cot, zeros], axis=1),
        ],
        axis=0,
    )
    dense_both = matmul_transposed(both, dense_full)
    dense_both = scatter_x(in_line_order([columns(dense_both, k) for k in range(4)], x))

    terms = jnp.stack(
        [
            dense_both[:group_rows] + to_tokens(expert_out * weight),
            dense_both[group_rows:] + to_tokens(expert_back),
        ]
    )
    terms = terms.astype(bf16).reshape(2, 8, -1, width).transpose(1, 0, 2, 3)
    arrived = exchange_tp(terms).astype(f32)
    arrived = arrived[:4] + arrived[4:]
    forward_total, backward_total = (
        jnp.concatenate([arrived[k, side] for k in range(4)], axis=1) for side in range(2)
    )
    mixed = (inputs + forward_total).astype(bf16)
    normed_cot = backward_total * norm_gain
    input_grad = (
        cotangent.astype(f32)
        + inverse * (normed_cot - scaled * jnp.mean(normed_cot * scaled, axis=1, keepdims=True))
    ).astype(bf16)
    return (mixed, input_grad)


def solution(mesh):
    return jax.shard_map(
        body,
        mesh=mesh,
        in_specs=(
            P(("ep", "tp"), None),
            P(),
            P("ep", "tp"),
            P("ep", "tp"),
            P("tp", "ep"),
            P("ep", None, "tp"),
            P("ep", None, "tp"),
            P("ep", "tp", None),
            P("ep", None),
            P("ep", None),
            P(("ep", "tp"), None),
        ),
        out_specs=(P(("ep", "tp"), None), P(("ep", "tp"), None)),
        check_vma=False,
    )
```

```python
import jax
import jax.numpy as jnp
from jax import lax
from jax.experimental import pallas as pl
from jax.experimental.pallas import tpu as pltpu
from jax.sharding import PartitionSpec as P

norm_eps = 1e-05
bf16 = jnp.bfloat16
f32 = jnp.float32


def silu_parts(pre):
    sigma = jax.nn.sigmoid(pre)
    return (pre * sigma, sigma * (1.0 + pre * (1.0 - sigma)))


def matmul(left, right):
    return jnp.dot(left, right, preferred_element_type=f32)


def matmul_transposed(left, right):
    return lax.dot_general(left, right, (((1,), (1,)), ((), ())), preferred_element_type=f32)


def prepare_kernel(tokens_ref, gain_ref, cotangent_ref, pieces_ref, inverse_ref):
    width = pieces_ref.shape[2] // 2
    inputs = tokens_ref[...].astype(f32)
    inverse = lax.rsqrt(jnp.mean(inputs * inputs, axis=1, keepdims=True) + norm_eps)
    inverse_ref[...] = inverse
    normed = (inputs * inverse * gain_ref[...]).astype(bf16)
    for k in range(pieces_ref.shape[0]):
        columns = slice(k % 4 * width, (k % 4 + 1) * width)
        pieces_ref[k, :, :width] = normed[:, columns]
        pieces_ref[k, :, width:] = cotangent_ref[:, columns]


def prepare(tokens, norm_gain, cotangent):
    rows, columns = tokens.shape
    return pl.pallas_call(
        prepare_kernel,
        out_shape=(
            jax.ShapeDtypeStruct((8, rows, columns // 2), bf16),
            jax.ShapeDtypeStruct((rows, 1), f32),
        ),
        compiler_params=pltpu.CompilerParams(vmem_limit_bytes=32 * 1024 * 1024),
        cost_estimate=pl.CostEstimate(
            flops=8 * rows * columns, bytes_accessed=10 * rows * columns, transcendentals=rows
        ),
    )(tokens, norm_gain[None], cotangent)


def shift_x(array, step):
    return lax.ppermute(
        array, "tp", [(y * 4 + x, y * 4 + (x + step) % 4) for y in range(2) for x in range(4)]
    )


offsets = (0, -1, 1, 2)


def line(x):
    return [lax.rem(x + 4 + step, 4) for step in offsets]


def send_near(own):
    return shift_x(own, 1), shift_x(own, -1)


def send_far(low, high):
    half = low.shape[0] // 2
    return jnp.concatenate([shift_x(low[:half], 1), shift_x(high[half:], -1)], axis=0)


def gather_x(own):
    low, high = send_near(own)
    return [own, low, high, send_far(low, high)]


def reduce_far(far):
    half = far.shape[0] // 2
    return shift_x(far[:half].astype(bf16), -1), shift_x(far[half:].astype(bf16), 1)


def reduce_near(own, low, high, from_high, from_low):
    half = own.shape[0] // 2
    low = jnp.concatenate([low[:half] + from_high.astype(f32), low[half:]], axis=0)
    high = jnp.concatenate([high[:half], high[half:] + from_low.astype(f32)], axis=0)
    return (
        own
        + shift_x(low.astype(bf16), -1).astype(f32)
        + shift_x(high.astype(bf16), 1).astype(f32)
    )


def scatter_x(parts):
    own, low, high, far = parts
    return reduce_near(own, low, high, *reduce_far(far))


def in_line_order(blocks, x):
    order = line(x)
    return [
        lax.select_n(order[k], *blocks) for k in range(4)
    ]


def in_line_order_inverse(blocks, x):
    own, low, high, far = blocks
    by_offset = [own, high, far, low]
    return [lax.select_n(lax.rem(k + 4 - x, 4), *by_offset) for k in range(4)]


def exchange_tp(blocks):
    return lax.all_to_all(blocks, "tp", split_axis=0, concat_axis=0, tiled=True)


def exchange(rows):
    experts = lax.axis_size("ep")
    return lax.all_to_all(
        rows.reshape(experts, -1, rows.shape[1]), "ep", split_axis=0, concat_axis=0, tiled=True
    ).reshape(rows.shape)


def slots(expert_ids, experts):
    route_expert = expert_ids.reshape(-1)
    onehot = (route_expert[:, None] == jnp.arange(experts, dtype=jnp.int32)[None, :]).astype(f32)
    routes = route_expert.shape[0]
    before = jnp.tril(jnp.ones((routes, routes), f32), -1)
    earlier = matmul(before.astype(bf16), onehot.astype(bf16))
    slot = jnp.sum(earlier * onehot, axis=1).astype(jnp.int32)
    return route_expert.reshape(-1, 2), slot.reshape(-1, 2)


def body(
    tokens,
    norm_gain,
    dense_gate,
    dense_up,
    dense_down,
    expert_gate,
    expert_up,
    expert_down,
    expert_ids,
    gate_weights,
    cotangent,
):
    experts = lax.axis_size("ep")
    group_rows = expert_ids.shape[0]
    capacity = 4 * group_rows // experts
    hidden_units = dense_gate.shape[1]
    inputs = tokens.astype(f32)
    pieces, inverse = prepare(tokens, norm_gain, cotangent)
    scaled = inputs * inverse

    me = lax.axis_index("tp")
    x = lax.rem(me, 4)
    width = tokens.shape[1] // 4

    def columns(array, k):
        return array[:, k * width : (k + 1) * width]

    group = exchange_tp(pieces).reshape(group_rows, -1)
    group, *dense_parts = lax.optimization_barrier((group, dense_gate, dense_up, dense_down))
    dense_own = jnp.concatenate([dense_parts[0], dense_parts[1], dense_parts[2].T], axis=1)
    dense_full = lax.all_gather(dense_own, "ep", axis=0, tiled=True)

    route_expert, slot = slots(expert_ids, experts)
    place = jnp.arange(experts * capacity, dtype=jnp.int32)[:, None]
    position = route_expert * capacity + slot
    pick, weight = None, None
    for k in range(2):
        chosen = position[None, :, k] == place
        chosen_weight = jnp.where(chosen, gate_weights[None, :, k], 0.0)
        pick = chosen if pick is None else pick | chosen
        weight = chosen_weight if weight is None else weight + chosen_weight
    weight = jnp.sum(weight, axis=1, keepdims=True)
    pick_f32 = pick.astype(f32)
    pick_bf16 = pick.astype(bf16)

    dense_rows = gather_x(group)
    rows_in = exchange(matmul(pick_bf16, group[:, :width]).astype(bf16))
    outgoing_cot = (matmul(pick_bf16, group[:, width:]) * weight).astype(bf16)
    def row_blocks(array):
        return in_line_order([array[k * width : (k + 1) * width] for k in range(4)], x)

    local_gate, local_up = row_blocks(expert_gate[0]), row_blocks(expert_up[0])
    local_down = in_line_order([columns(expert_down[0], k) for k in range(4)], x)
    rows_in, dense_rows, local_gate, local_up, local_down = lax.optimization_barrier(
        (rows_in, dense_rows, local_gate, local_up, local_down)
    )
    low, high = send_near(rows_in)
    rows_cot = exchange(outgoing_cot)
    far = send_far(low, high)
    rows_in = [rows_in, low, high]
    def forward_terms(k):
        return matmul(expert_hidden, local_down[k])

    def backward_terms(k):
        return matmul_transposed(expert_gate_cot, local_gate[k]) + matmul_transposed(
            expert_up_cot, local_up[k]
        )

    expert_gate_pre = sum(matmul(rows_in[k], local_gate[k]) for k in range(3))
    expert_up_pre = sum(matmul(rows_in[k], local_up[k]) for k in range(3))
    expert_gate_pre, expert_up_pre, far = lax.optimization_barrier(
        (expert_gate_pre, expert_up_pre, far)
    )
    expert_gate_pre += matmul(far, local_gate[3])
    expert_up_pre += matmul(far, local_up[3])
    expert_active, expert_slope = silu_parts(expert_gate_pre)
    expert_hidden = (expert_active * expert_up_pre).astype(bf16)
    forward_far = reduce_far(forward_terms(3))
    rows_cot, forward_far = lax.optimization_barrier((rows_cot, forward_far))
    cot_low, cot_high = send_near(rows_cot)
    cot_far = send_far(cot_low, cot_high)
    expert_out = reduce_near(*[forward_terms(k) for k in range(3)], *forward_far).astype(bf16)

    rows_cot = [rows_cot, cot_low, cot_high]
    expert_hidden_cot = sum(matmul_transposed(rows_cot[k], local_down[k]) for k in range(3))
    expert_hidden_cot, cot_far = lax.optimization_barrier((expert_hidden_cot, cot_far))
    expert_hidden_cot += matmul_transposed(cot_far, local_down[3])
    expert_gate_cot = (expert_hidden_cot * expert_up_pre * expert_slope).astype(bf16)
    expert_up_cot = (expert_hidden_cot * expert_active).astype(bf16)
    back_far = backward_terms(3).astype(bf16)
    back_far = reduce_far(back_far)
    expert_out, back_far = lax.optimization_barrier((expert_out, back_far))
    expert_out = exchange(expert_out)

    def to_tokens(slot_rows):
        return lax.dot_general(
            pick_f32,
            slot_rows,
            (((0,), (0,)), ((), ())),
            precision=lax.Precision.HIGHEST,
            preferred_element_type=f32,
        )

    dense_rows = jnp.concatenate(
        [
            jnp.concatenate([rows[:, :width], rows[:, width:]], axis=0)
            for rows in in_line_order_inverse(dense_rows, x)
        ],
        axis=1,
    )
    pre = matmul(dense_rows, dense_full)
    gate_pre = pre[:group_rows, :hidden_units]
    up_pre = pre[:group_rows, hidden_units : 2 * hidden_units]
    hidden_cot = pre[group_rows:, 2 * hidden_units :]
    active, slope = silu_parts(gate_pre)
    hidden = (active * up_pre).astype(bf16)
    gate_cot = (hidden_cot * up_pre * slope).astype(bf16)
    up_cot = (hidden_cot * active).astype(bf16)
    zeros = jnp.zeros_like(hidden)
    both = jnp.concatenate(
        [
            jnp.concatenate([zeros, zeros, hidden], axis=1),
            jnp.concatenate([gate_cot, up_cot, zeros], axis=1),
        ],
        axis=0,
    )
    dense_both = matmul_transposed(both, dense_full)
    expert_back = reduce_near(*[backward_terms(k) for k in range(3)], *back_far).astype(bf16)
    expert_out, expert_back, dense_both = lax.optimization_barrier(
        (expert_out, expert_back, dense_both)
    )
    expert_out = expert_out.astype(f32)
    expert_back = exchange(expert_back).astype(f32)
    dense_both = scatter_x(in_line_order([columns(dense_both, k) for k in range(4)], x))

    terms = jnp.stack(
        [
            dense_both[:group_rows] + to_tokens(expert_out * weight),
            dense_both[group_rows:] + to_tokens(expert_back),
        ]
    )
    terms = terms.astype(bf16).reshape(2, 8, -1, width).transpose(1, 0, 2, 3)
    arrived = exchange_tp(terms).astype(f32)
    arrived = arrived[:4] + arrived[4:]
    forward_total, backward_total = (
        jnp.concatenate([arrived[k, side] for k in range(4)], axis=1) for side in range(2)
    )
    mixed = (inputs + forward_total).astype(bf16)
    normed_cot = backward_total * norm_gain
    input_grad = (
        cotangent.astype(f32)
        + inverse * (normed_cot - scaled * jnp.mean(normed_cot * scaled, axis=1, keepdims=True))
    ).astype(bf16)
    return (mixed, input_grad)


def solution(mesh):
    return jax.shard_map(
        body,
        mesh=mesh,
        in_specs=(
            P(("ep", "tp"), None),
            P(),
            P("ep", "tp"),
            P("ep", "tp"),
            P("tp", "ep"),
            P("ep", None, "tp"),
            P("ep", None, "tp"),
            P("ep", "tp", None),
            P("ep", None),
            P("ep", None),
            P(("ep", "tp"), None),
        ),
        out_specs=(P(("ep", "tp"), None), P(("ep", "tp"), None)),
        check_vma=False,
    )
```

```python
import jax
import jax.numpy as jnp
from jax import lax
from jax.experimental import pallas as pl
from jax.experimental.pallas import tpu as pltpu
from jax.sharding import PartitionSpec as P

norm_eps = 1e-05
bf16 = jnp.bfloat16
f32 = jnp.float32


def silu_parts(pre):
    sigma = jax.nn.sigmoid(pre)
    return (pre * sigma, sigma * (1.0 + pre * (1.0 - sigma)))


def matmul(left, right):
    return jnp.dot(left, right, preferred_element_type=f32)


def matmul_transposed(left, right):
    return lax.dot_general(left, right, (((1,), (1,)), ((), ())), preferred_element_type=f32)


def prepare_kernel(tokens_ref, gain_ref, cotangent_ref, pieces_ref, inverse_ref):
    width = pieces_ref.shape[2] // 2
    inputs = tokens_ref[...].astype(f32)
    inverse = lax.rsqrt(jnp.mean(inputs * inputs, axis=1, keepdims=True) + norm_eps)
    inverse_ref[...] = inverse
    normed = (inputs * inverse * gain_ref[...]).astype(bf16)
    for k in range(pieces_ref.shape[0]):
        columns = slice(k % 4 * width, (k % 4 + 1) * width)
        pieces_ref[k, :, :width] = normed[:, columns]
        pieces_ref[k, :, width:] = cotangent_ref[:, columns]


def prepare(tokens, norm_gain, cotangent):
    rows, columns = tokens.shape
    return pl.pallas_call(
        prepare_kernel,
        out_shape=(
            jax.ShapeDtypeStruct((8, rows, columns // 2), bf16),
            jax.ShapeDtypeStruct((rows, 1), f32),
        ),
        compiler_params=pltpu.CompilerParams(vmem_limit_bytes=32 * 1024 * 1024),
        cost_estimate=pl.CostEstimate(
            flops=8 * rows * columns, bytes_accessed=10 * rows * columns, transcendentals=rows
        ),
    )(tokens, norm_gain[None], cotangent)


def shift_x(array, step):
    return lax.ppermute(
        array, "tp", [(y * 4 + x, y * 4 + (x + step) % 4) for y in range(2) for x in range(4)]
    )


offsets = (0, -1, 1, 2)


def line(x):
    return [lax.rem(x + 4 + step, 4) for step in offsets]


def send_near(own):
    return shift_x(own, 1), shift_x(own, -1)


def send_far(low, high):
    half = low.shape[0] // 2
    return jnp.concatenate([shift_x(low[:half], 1), shift_x(high[half:], -1)], axis=0)


def gather_x(own):
    low, high = send_near(own)
    return [own, low, high, send_far(low, high)]


def reduce_far(far):
    half = far.shape[0] // 2
    return shift_x(far[:half].astype(bf16), -1), shift_x(far[half:].astype(bf16), 1)


def send_near_terms(own, low, high, from_high, from_low):
    half = own.shape[0] // 2
    low = jnp.concatenate([low[:half] + from_high.astype(f32), low[half:]], axis=0)
    high = jnp.concatenate([high[:half], high[half:] + from_low.astype(f32)], axis=0)
    return own, shift_x(low.astype(bf16), -1), shift_x(high.astype(bf16), 1)


def reduce_near(own, low, high, from_high, from_low):
    own, low, high = send_near_terms(own, low, high, from_high, from_low)
    return own + low.astype(f32) + high.astype(f32)


def scatter_x(parts):
    own, low, high, far = parts
    return reduce_near(own, low, high, *reduce_far(far))


def in_line_order(blocks, x):
    order = line(x)
    return [
        lax.select_n(order[k], *blocks) for k in range(4)
    ]


def in_line_order_inverse(blocks, x):
    own, low, high, far = blocks
    by_offset = [own, high, far, low]
    return [lax.select_n(lax.rem(k + 4 - x, 4), *by_offset) for k in range(4)]


def exchange_tp(blocks):
    return lax.all_to_all(blocks, "tp", split_axis=0, concat_axis=0, tiled=True)


def exchange(rows):
    experts = lax.axis_size("ep")
    return lax.all_to_all(
        rows.reshape(experts, -1, rows.shape[1]), "ep", split_axis=0, concat_axis=0, tiled=True
    ).reshape(rows.shape)


def slots(expert_ids, experts):
    route_expert = expert_ids.reshape(-1)
    onehot = (route_expert[:, None] == jnp.arange(experts, dtype=jnp.int32)[None, :]).astype(f32)
    routes = route_expert.shape[0]
    before = jnp.tril(jnp.ones((routes, routes), f32), -1)
    earlier = matmul(before.astype(bf16), onehot.astype(bf16))
    slot = jnp.sum(earlier * onehot, axis=1).astype(jnp.int32)
    return route_expert.reshape(-1, 2), slot.reshape(-1, 2)


def body(
    tokens,
    norm_gain,
    dense_gate,
    dense_up,
    dense_down,
    expert_gate,
    expert_up,
    expert_down,
    expert_ids,
    gate_weights,
    cotangent,
):
    experts = lax.axis_size("ep")
    group_rows = expert_ids.shape[0]
    capacity = 4 * group_rows // experts
    hidden_units = dense_gate.shape[1]
    inputs = tokens.astype(f32)
    pieces, inverse = prepare(tokens, norm_gain, cotangent)
    scaled = inputs * inverse

    me = lax.axis_index("tp")
    x = lax.rem(me, 4)
    width = tokens.shape[1] // 4

    def columns(array, k):
        return array[:, k * width : (k + 1) * width]

    group = exchange_tp(pieces).reshape(group_rows, -1)
    group, *dense_parts = lax.optimization_barrier((group, dense_gate, dense_up, dense_down))
    dense_own = jnp.concatenate([dense_parts[0], dense_parts[1], dense_parts[2].T], axis=1)
    dense_full = lax.all_gather(dense_own, "ep", axis=0, tiled=True)

    route_expert, slot = slots(expert_ids, experts)
    place = jnp.arange(experts * capacity, dtype=jnp.int32)[:, None]
    position = route_expert * capacity + slot
    pick, weight = None, None
    for k in range(2):
        chosen = position[None, :, k] == place
        chosen_weight = jnp.where(chosen, gate_weights[None, :, k], 0.0)
        pick = chosen if pick is None else pick | chosen
        weight = chosen_weight if weight is None else weight + chosen_weight
    weight = jnp.sum(weight, axis=1, keepdims=True)
    pick_f32 = pick.astype(f32)
    pick_bf16 = pick.astype(bf16)

    dense_rows = gather_x(group)
    rows_in = exchange(matmul(pick_bf16, group[:, :width]).astype(bf16))
    outgoing_cot = (matmul(pick_bf16, group[:, width:]) * weight).astype(bf16)
    def row_blocks(array):
        return in_line_order([array[k * width : (k + 1) * width] for k in range(4)], x)

    local_gate, local_up = row_blocks(expert_gate[0]), row_blocks(expert_up[0])
    local_down = in_line_order([columns(expert_down[0], k) for k in range(4)], x)
    rows_in, dense_rows, local_gate, local_up, local_down = lax.optimization_barrier(
        (rows_in, dense_rows, local_gate, local_up, local_down)
    )
    low, high = send_near(rows_in)
    rows_cot = exchange(outgoing_cot)
    far = send_far(low, high)
    rows_in = [rows_in, low, high]
    def forward_terms(k):
        return matmul(expert_hidden, local_down[k])

    def backward_terms(k):
        return matmul_transposed(expert_gate_cot, local_gate[k]) + matmul_transposed(
            expert_up_cot, local_up[k]
        )

    expert_gate_pre = sum(matmul(rows_in[k], local_gate[k]) for k in range(3))
    expert_up_pre = sum(matmul(rows_in[k], local_up[k]) for k in range(3))
    expert_gate_pre, expert_up_pre, far = lax.optimization_barrier(
        (expert_gate_pre, expert_up_pre, far)
    )
    expert_gate_pre += matmul(far, local_gate[3])
    expert_up_pre += matmul(far, local_up[3])
    expert_active, expert_slope = silu_parts(expert_gate_pre)
    expert_hidden = (expert_active * expert_up_pre).astype(bf16)
    forward_far = reduce_far(forward_terms(3))
    rows_cot, forward_far = lax.optimization_barrier((rows_cot, forward_far))
    cot_low, cot_high = send_near(rows_cot)
    cot_far = send_far(cot_low, cot_high)
    expert_out = reduce_near(*[forward_terms(k) for k in range(3)], *forward_far).astype(bf16)

    rows_cot = [rows_cot, cot_low, cot_high]
    expert_hidden_cot = sum(matmul_transposed(rows_cot[k], local_down[k]) for k in range(3))
    expert_hidden_cot, cot_far = lax.optimization_barrier((expert_hidden_cot, cot_far))
    expert_hidden_cot += matmul_transposed(cot_far, local_down[3])
    expert_gate_cot = (expert_hidden_cot * expert_up_pre * expert_slope).astype(bf16)
    expert_up_cot = (expert_hidden_cot * expert_active).astype(bf16)
    back_far = backward_terms(3).astype(bf16)
    back_far = reduce_far(back_far)
    expert_out, back_far = lax.optimization_barrier((expert_out, back_far))
    expert_out = exchange(expert_out)

    def to_tokens(slot_rows):
        return lax.dot_general(
            pick_f32,
            slot_rows,
            (((0,), (0,)), ((), ())),
            precision=lax.Precision.HIGHEST,
            preferred_element_type=f32,
        )

    dense_rows = jnp.concatenate(
        [
            jnp.concatenate([rows[:, :width], rows[:, width:]], axis=0)
            for rows in in_line_order_inverse(dense_rows, x)
        ],
        axis=1,
    )
    pre = matmul(dense_rows, dense_full)
    gate_pre = pre[:group_rows, :hidden_units]
    up_pre = pre[:group_rows, hidden_units : 2 * hidden_units]
    hidden_cot = pre[group_rows:, 2 * hidden_units :]
    active, slope = silu_parts(gate_pre)
    hidden = (active * up_pre).astype(bf16)
    gate_cot = (hidden_cot * up_pre * slope).astype(bf16)
    up_cot = (hidden_cot * active).astype(bf16)
    zeros = jnp.zeros_like(hidden)
    both = jnp.concatenate(
        [
            jnp.concatenate([zeros, zeros, hidden], axis=1),
            jnp.concatenate([gate_cot, up_cot, zeros], axis=1),
        ],
        axis=0,
    )
    dense_both = matmul_transposed(both, dense_full)
    own_back, *arrived_back = send_near_terms(
        *[backward_terms(k) for k in range(3)], *back_far
    )
    expert_out, arrived_back, dense_both = lax.optimization_barrier(
        (expert_out, arrived_back, dense_both)
    )
    expert_back = (
        own_back + arrived_back[0].astype(f32) + arrived_back[1].astype(f32)
    ).astype(bf16)
    expert_out = expert_out.astype(f32)
    expert_back = exchange(expert_back).astype(f32)
    dense_both = scatter_x(in_line_order([columns(dense_both, k) for k in range(4)], x))

    terms = jnp.stack(
        [
            dense_both[:group_rows] + to_tokens(expert_out * weight),
            dense_both[group_rows:] + to_tokens(expert_back),
        ]
    )
    terms = terms.astype(bf16).reshape(2, 8, -1, width).transpose(1, 0, 2, 3)
    arrived = exchange_tp(terms).astype(f32)
    arrived = arrived[:4] + arrived[4:]
    forward_total, backward_total = (
        jnp.concatenate([arrived[k, side] for k in range(4)], axis=1) for side in range(2)
    )
    mixed = (inputs + forward_total).astype(bf16)
    normed_cot = backward_total * norm_gain
    input_grad = (
        cotangent.astype(f32)
        + inverse * (normed_cot - scaled * jnp.mean(normed_cot * scaled, axis=1, keepdims=True))
    ).astype(bf16)
    return (mixed, input_grad)


def solution(mesh):
    return jax.shard_map(
        body,
        mesh=mesh,
        in_specs=(
            P(("ep", "tp"), None),
            P(),
            P("ep", "tp"),
            P("ep", "tp"),
            P("tp", "ep"),
            P("ep", None, "tp"),
            P("ep", None, "tp"),
            P("ep", "tp", None),
            P("ep", None),
            P("ep", None),
            P(("ep", "tp"), None),
        ),
        out_specs=(P(("ep", "tp"), None), P(("ep", "tp"), None)),
        check_vma=False,
    )
```
